512 devices in a mesh: frame: 8 (over x, core), row: 8 (over z_lo), col: 8 (over y, z_hi).
Axes of the slice: x: 4, y: 4, z: 16 (z_hi: 2, z_lo: 8; z = z_hi * 8 + z_lo), core: 2. Of those that a mesh axis runs over, the one named last changes fastest.
Arguments:
- queries: bfloat16 [16, 64, 64, 2240], P('frame', 'row', 'col'), may hold values from -5 to 5
- keys: bfloat16 [16, 64, 64, 2240], P('frame', 'row', 'col'), may hold values from -120 to 120
- values: bfloat16 [16, 64, 64, 2240], P('frame', 'row', 'col'), may hold values from -12 to 12
- hidden: bfloat16 [16, 64, 64, 5632], P('frame', 'row', 'col'), may hold values from -5 to 5
- conv_weight: float32 [9, 5632], replicated, may hold values from -2 to 2
- conv_bias: float32 [5632], replicated, may hold values from -2.5 to 2.5
Outputs:
- attended: bfloat16 [16, 64, 64, 2240], P('frame', 'row', 'col')
- gated: bfloat16 [16, 64, 64, 2816], P('frame', 'row', 'col')
The draws below stay inside these ranges and needn't reach their ends.
All inputs are finite; a program needn't handle non-finite values.
Results may differ from the reference program's by a relative error of at most 0.0004.
Values may be sent and summed in bfloat16 or wider, within the bound.
A program may use at most 64 MiB of HBM per device.

```python
import math
import jax
import jax.numpy as jnp
from jax import lax

HEADS = 70
HD = 32
HU = 2816
WIDTH = 2240
CONV_CH = 5632
FRAMES = 16
ROWS = 64
COLS = 64
N_FRAME = 8


def draw_keys(key, part):
    key = jax.random.fold_in(key, 11)
    first, second, third = jax.random.split(key, 3)
    base = jnp.clip(jax.random.normal(first, (FRAMES, ROWS, COLS, HEADS * HD), jnp.float32), -4.0, 4.0)
    top = math.log(10.0)
    scale = jnp.exp(jax.random.uniform(second, (FRAMES, ROWS, COLS, 1), jnp.float32, 0.0, top))
    region = jax.random.uniform(third, (FRAMES, (ROWS + 3) // 4, (COLS + 3) // 4, HEADS * HD), jnp.float32, 0.0, math.log(1000.0))
    region = jnp.repeat(jnp.repeat(region, 4, axis=1), 4, axis=2)[:, :ROWS, :COLS]
    return (base * scale * jnp.exp(-region)).astype(jnp.bfloat16)


def draw_values(key, part):
    key = jax.random.fold_in(key, 23)
    k_noise, k_frame, k_region, k_channel = jax.random.split(key, 4)
    shape = (FRAMES, ROWS, COLS, HEADS * HD)
    noise = 0.5 * jnp.clip(jax.random.normal(k_noise, shape, jnp.float32), -3.0, 3.0)
    frame_part = jnp.clip(jax.random.normal(k_frame, (FRAMES, 1, 1, HEADS * HD), jnp.float32), -3.0, 3.0)
    coarse = jnp.clip(jax.random.normal(k_region, (FRAMES, (ROWS + 3) // 4, (COLS + 3) // 4, HEADS * HD), jnp.float32), -3.0, 3.0)
    coarse = jnp.repeat(jnp.repeat(coarse, 4, axis=1), 4, axis=2)[:, :ROWS, :COLS]
    channel = jnp.clip(jax.random.normal(k_channel, (1, 1, 1, HEADS * HD), jnp.float32), -3.0, 3.0)
    return (noise + frame_part + 1.5 * coarse + channel).astype(jnp.bfloat16)


def level_of(stream_key, extent, pieces, least, top_value):
    def one(dim, blocks):
        steps = jax.random.uniform(jax.random.fold_in(jax.random.fold_in(stream_key, 6), dim), (blocks,), jnp.float32, least / len(pieces), top_value / len(pieces))
        return jnp.repeat(jnp.exp(steps), extent[dim] // blocks).reshape((-1,) + (1,) * (len(extent) - dim - 1))

    level = one(*pieces[0])
    for cut in pieces[1:]:
        level = level * one(*cut)
    return level


def scatter_about(rng, dims, spread, most, pieces=(), dtype=jnp.bfloat16):
    gain = level_of(rng, dims, pieces, -0.22, 0.18) if pieces else 1.0
    entries = jax.random.normal(rng, dims, jnp.float32) * spread * gain
    return jnp.minimum(jnp.maximum(entries, -most), most).astype(dtype)


def setup_inputs(seed: int = 0) -> dict:
    key_of = jax.random.split(jax.random.key(seed), 7)
    return {
        "queries": scatter_about(key_of[0], (FRAMES, ROWS, COLS, WIDTH), 1.0, 5.0, ((0, 8), (1, 8), (2, 8))),
        "keys": draw_keys(jax.random.fold_in(key_of[6], 71), 0),
        "values": draw_values(jax.random.fold_in(key_of[6], 71), 0),
        "hidden": scatter_about(key_of[3], (FRAMES, ROWS, COLS, CONV_CH), 1.0, 5.0, ((0, 8), (1, 8), (2, 8))),
        "conv_weight": scatter_about(key_of[4], (9, CONV_CH), 9 ** -0.5, 2.0, (), jnp.float32),
        "conv_bias": scatter_about(key_of[5], (CONV_CH,), 0.5, 2.5, (), jnp.float32),
    }


EPS = 1e-6
HIGH = lax.Precision.HIGHEST


def block_state(pair):
    key_block, value_block = pair
    kpos = jnp.maximum(key_block.astype(jnp.float32), 0.0).reshape(-1, HEADS, HD)
    vals = value_block.astype(jnp.float32).reshape(-1, HEADS, HD)
    state = jnp.einsum('thd,the->hde', kpos, vals, precision=HIGH)
    return state, jnp.sum(kpos, axis=0)


def block_output(triple):
    query_block, prefix, zprefix = triple
    qpos = jnp.maximum(query_block.astype(jnp.float32), 0.0).reshape(-1, HEADS, HD)
    numer = jnp.einsum('thd,hde->the', qpos, prefix, precision=HIGH)
    denom = jnp.einsum('thd,hd->th', qpos, zprefix, precision=HIGH) + EPS
    return (numer / denom[..., None]).reshape(-1, WIDTH).astype(jnp.bfloat16)


def reference(queries, keys, values, hidden, conv_weight, conv_bias):
    key_blocks = keys.reshape(N_FRAME, -1, WIDTH)
    value_blocks = values.reshape(N_FRAME, -1, WIDTH)
    query_blocks = queries.reshape(N_FRAME, -1, WIDTH)
    states, ksums = lax.map(block_state, (key_blocks, value_blocks))
    prefix = jnp.cumsum(states, axis=0)
    zprefix = jnp.cumsum(ksums, axis=0)
    attended = lax.map(block_output, (query_blocks, prefix, zprefix)).reshape(FRAMES, ROWS, COLS, WIDTH)

    def conv_frame(frame):
        padded = jnp.pad(frame.astype(jnp.float32), ((1, 1), (1, 1), (0, 0)))
        total = jnp.zeros((ROWS, COLS, CONV_CH), jnp.float32) + conv_bias
        for shift_r in range(3):
            for shift_c in range(3):
                total = total + conv_weight[3 * shift_r + shift_c] * padded[shift_r:shift_r + ROWS, shift_c:shift_c + COLS]
        return (total[..., :HU] * jax.nn.silu(total[..., HU:])).astype(jnp.bfloat16)

    gated = lax.map(conv_frame, hidden)
    return attended, gated
```

```python
import jax
import jax.numpy as jnp
from jax import lax
from jax.experimental import pallas as pl
from jax.experimental.pallas import tpu as pltpu
from jax.sharding import PartitionSpec as P

MESH = pl.DeviceIdType.MESH
F32, BF16 = jnp.float32, jnp.bfloat16

HEADS = 70
HD = 32
WIDTH = HEADS * HD
HU = 2816
CH = 2 * HU
EPS = 1e-6

LANES = 128
FULL_TILES = WIDTH // LANES
TAIL = WIDTH - FULL_TILES * LANES
TILES = FULL_TILES + 1
KSUM = 4 * TILES
UNITS = 80
QUARTER = UNITS // 4
PIECE = QUARTER // 4

CHUNK = 256
CHUNKS = HU // CHUNK
FIRST, SECOND = 3, 4


def iota(shape, dim):
    return lax.broadcasted_iota(jnp.int32, shape, dim)


def kernel(
    q_hbm, k_hbm, v_hbm, h_hbm, w_hbm, b_hbm,
    att, gated,
    q, k, v, h, w, bias,
    state, sums, y_in, y_sum, za_in, za_sum, zb_in, zb_sum, x_in, prefix,
    col_out, col_in, row_in, cor_out, cor_in, conv, pick, spread,
    local_sem, row_s, row_r, col_s, col_r, cor_s, cor_r,
    ry_s, ry_r, ra_s, ra_r, rb_s, rb_r, x_s, x_r, ga_s, ga_r, gy_s, gy_r,
):
    f, r, c = lax.axis_index("frame"), lax.axis_index("row"), lax.axis_index("col")
    y, z = c // 2, (c % 2) * 8 + r
    ia = r % 4

    def y_peer(j):
        return (f, r, ((y + j) % 4) * 2 + c % 2)

    def za_peer(j):
        return (f, (r // 4) * 4 + (ia + j) % 4, c)

    def zb_peer(j):
        far = (z + 4 * j) % 16
        return (f, far % 8, y * 2 + far // 8)

    def remote(src, dst, s, rr, to):
        return pltpu.make_async_remote_copy(
            src_ref=src, dst_ref=dst, send_sem=s, recv_sem=rr, device_id=to, device_id_type=MESH
        )

    barrier = pltpu.get_barrier_semaphore()

    def greet(to):
        pl.semaphore_signal(barrier, inc=1, device_id=to, device_id_type=MESH)

    for ok, to in ((c > 0, (f, r, c - 1)), (c < 7, (f, r, c + 1)), (r > 0, (f, r - 1, c)), (r < 7, (f, r + 1, c))):
        pl.when(ok)(lambda to=to: greet(to))
    for j in (1, 2, 3):
        greet(y_peer(j))
        greet(za_peer(j))
        greet(zb_peer(j))
    for j in range(1, 8):
        greet(((f + j) % 8, r, c))

    loads = [
        pltpu.make_async_copy(src, dst, local_sem.at[n])
        for n, (src, dst) in enumerate(((h_hbm, h), (k_hbm, k), (v_hbm, v), (w_hbm, w), (b_hbm, bias), (q_hbm, q)))
    ]
    for load in loads:
        load.start()

    tok, row = iota((32, 128), 1), iota((32, 128), 0)
    pick_cols = ((tok // 8 == row % 16) & (tok % 8 == jnp.where(row < 16, 0, 7))).astype(F32).astype(BF16)

    loads[0].wait()

    def take_columns(jc, carry):
        for half in (0, 1):
            lanes = pl.ds(pl.multiple_of(half * HU + jc * CHUNK, LANES), CHUNK)
            part = h[:, :, :, lanes].astype(F32).reshape(128, CHUNK).astype(BF16)
            got = jnp.dot(pick_cols, part, preferred_element_type=F32).astype(BF16)
            col_out[0, jc, :, half * CHUNK : (half + 1) * CHUNK] = got[:16]
            col_out[1, jc, :, half * CHUNK : (half + 1) * CHUNK] = got[16:]
        return carry

    lax.fori_loop(0, CHUNKS, take_columns, 0)

    peers = 16 + (c > 0).astype(jnp.int32) + (c < 7).astype(jnp.int32) + (r > 0).astype(jnp.int32) + (r < 7).astype(jnp.int32)
    pl.semaphore_wait(barrier, peers)

    sends = (
        (c > 0, lambda jc: remote(col_out.at[0, jc], col_in.at[1, jc], col_s.at[0, jc], col_r.at[1, jc], (f, r, c - 1))),
        (c < 7, lambda jc: remote(col_out.at[1, jc], col_in.at[0, jc], col_s.at[1, jc], col_r.at[0, jc], (f, r, c + 1))),
    )
    up_row = remote(h.at[:, 0], row_in.at[1], row_s.at[0], row_r.at[1], (f, r - 1, c))
    down_row = remote(h.at[:, 7], row_in.at[0], row_s.at[1], row_r.at[0], (f, r + 1, c))

    def up_corner(jc):
        return remote(cor_out.at[0, jc], cor_in.at[1, jc], cor_s.at[0, jc], cor_r.at[1, jc], (f, r - 1, c))

    def down_corner(jc):
        return remote(cor_out.at[1, jc], cor_in.at[0, jc], cor_s.at[1, jc], cor_r.at[0, jc], (f, r + 1, c))

    def send_columns(first, last):
        def step(jc, carry):
            for ok, copy in sends:
                pl.when(ok)(lambda copy=copy: copy(jc).start())
            return carry

        lax.fori_loop(first, last, step, 0)

    pl.when(r > 0)(lambda: up_row.start())
    pl.when(r < 7)(lambda: down_row.start())
    send_columns(0, FIRST)

    @pl.when(c == 0)
    def _():
        col_in[0] = jnp.zeros(col_in.shape[1:], BF16)

    @pl.when(c == 7)
    def _():
        col_in[1] = jnp.zeros(col_in.shape[1:], BF16)

    @pl.when(r == 0)
    def _():
        row_in[0] = jnp.zeros(row_in.shape[1:], BF16)
        cor_in[0] = jnp.zeros(cor_in.shape[1:], BF16)

    @pl.when(r == 7)
    def _():
        row_in[1] = jnp.zeros(row_in.shape[1:], BF16)
        cor_in[1] = jnp.zeros(cor_in.shape[1:], BF16)

    loads[1].wait()
    loads[2].wait()
    sums[...] = jnp.zeros_like(sums)
    state[pl.ds(KSUM, UNITS - KSUM)] = jnp.zeros((UNITS - KSUM, 8, LANES), F32)
    head_of_lane = iota((HD, LANES), 1) // HD

    def state_tile(j, kk, vv):
        kk = jnp.maximum(kk, 0.0)
        full = lax.dot_general(kk.astype(BF16), vv.astype(BF16), (((0,), (0,)), ((), ())), preferred_element_type=F32)
        tile = jnp.zeros((HD, LANES), F32)
        for g in range(4):
            tile = tile + jnp.where(head_of_lane == g, full[g * HD : (g + 1) * HD], 0.0)
        state[pl.ds(4 * j, 4)] = tile.reshape(4, 8, LANES)
        sums[pl.ds(j, 1), :] = jnp.sum(kk, axis=0, keepdims=True)

    def tail_of(ref):
        part = ref[:, :, :, FULL_TILES * LANES :].astype(F32).reshape(128, TAIL)
        return jnp.concatenate([part, jnp.zeros((128, LANES - TAIL), F32)], axis=1)

    def tile_of(ref, j):
        return ref[:, :, :, pl.ds(pl.multiple_of(j * LANES, LANES), LANES)].astype(F32).reshape(128, LANES)

    def state_step(j, carry):
        state_tile(j, tile_of(k, j), tile_of(v, j))
        return carry

    lax.fori_loop(0, FULL_TILES, state_step, 0)
    state_tile(FULL_TILES, tail_of(k), tail_of(v))
    state[pl.ds(KSUM, 3)] = sums[...].reshape(3, 8, LANES)

    reduce_y = [
        remote(state.at[pl.ds(QUARTER * ((y + j) % 4), QUARTER)], y_in.at[j - 1], ry_s.at[j - 1], ry_r.at[j - 1], y_peer(j))
        for j in (1, 2, 3)
    ]
    for copy in reduce_y:
        copy.start()

    tok, src = iota((128, 64), 0), iota((128, 64), 1)
    tf, tr, tc = tok // 64, (tok // 8) % 8, tok % 8
    side = jnp.where(tc == 7, 1, 0)
    edge = (tc == 0) | (tc == 7)
    for t in range(4):
        for a in range(3):
            at = tr + a - 1
            want = jnp.where(at < 0, 32 + t * 4 + side * 2 + tf, jnp.where(at > 7, 48 + t * 4 + side * 2 + tf, side * 16 + tf * 8 + at))
            spread[t, a * 128 : (a + 1) * 128, :] = (edge & (src == want)).astype(F32).astype(BF16)
    to, frm = iota((32, 32), 0), iota((32, 32), 1)
    for t in range(4):
        o = to % 16
        want = ((o % 4) // 2) * 16 + (o % 2) * 8 + jnp.where(to < 16, 0, 7)
        pick[t] = ((o // 4 == t) & (frm == want)).astype(F32).astype(BF16)

    loads[3].wait()
    loads[4].wait()
    pl.when(r < 7)(lambda: up_row.wait_recv())
    pl.when(r > 0)(lambda: down_row.wait_recv())

    sub = iota((8, LANES), 0)

    def conv_tile(n, carry):
        lanes = pl.ds(pl.multiple_of(n * LANES, LANES), LANES)
        x = h[:, :, :, lanes].astype(F32)
        above = row_in[0, :, :, lanes].astype(F32)
        below = row_in[1, :, :, lanes].astype(F32)
        x = jnp.concatenate([above[:, None], x, below[:, None]], axis=1)
        wt = [jnp.broadcast_to(w[m : m + 1, lanes], (8, LANES)) for m in range(9)]
        mid, left, right = (jnp.broadcast_to(bias[0:1, lanes], (8, LANES)), 0.0, 0.0)
        for a in range(3):
            rows = x[:, a : a + 8]
            left = left + rows * jnp.where(sub == 7, 0.0, wt[3 * a])
            mid = mid + rows * wt[3 * a + 1]
            right = right + rows * jnp.where(sub == 0, 0.0, wt[3 * a + 2])
        left = pltpu.roll(left.reshape(16, 8, LANES), 1, 1)
        right = pltpu.roll(right.reshape(16, 8, LANES), 7, 1)
        conv[:, :, lanes] = mid.reshape(16, 8, LANES) + left + right
        return carry

    lax.fori_loop(0, CH // LANES, conv_tile, 0)

    mine = state[pl.ds(QUARTER * y, QUARTER)]
    for j, copy in enumerate(reduce_y):
        copy.wait_recv()
        mine = mine + y_in[j]
    y_sum[...] = mine
    reduce_a = [
        remote(y_sum.at[pl.ds(PIECE * ((ia + j) % 4), PIECE)], za_in.at[j - 1], ra_s.at[j - 1], ra_r.at[j - 1], za_peer(j))
        for j in (1, 2, 3)
    ]
    for copy in reduce_a:
        copy.start()
    mine = y_sum[pl.ds(PIECE * ia, PIECE)]
    for j, copy in enumerate(reduce_a):
        copy.wait_recv()
        mine = mine + za_in[j]
    za_sum[...] = mine
    reduce_b = [remote(za_sum, zb_in.at[j - 1], rb_s.at[j - 1], rb_r.at[j - 1], zb_peer(j)) for j in (1, 2, 3)]
    for copy in reduce_b:
        copy.start()
    mine = za_sum[...]
    for j, copy in enumerate(reduce_b):
        copy.wait_recv()
        mine = mine + zb_in[j]
    zb_sum[...] = mine

    def to_later(b):
        return remote(zb_sum, x_in.at[f], x_s.at[b], x_r.at[f], (b, r, c))

    def from_earlier(b):
        return remote(zb_sum, x_in.at[b], x_s.at[b], x_r.at[b], (b, r, c))

    for b in range(1, 8):
        pl.when(f < b)(lambda b=b: to_later(b).start())
    send_columns(FIRST, SECOND)

    def add_earlier(b, total):
        from_earlier(b).wait_recv()
        return total + x_in[b]

    here = pl.ds(QUARTER * y + PIECE * ia, PIECE)
    prefix[here] = lax.fori_loop(0, f, add_earlier, zb_sum[...])

    gather_a = [remote(prefix.at[here], prefix.at[here], ga_s.at[j - 1], ga_r.at[j - 1], za_peer(j)) for j in (1, 2, 3)]
    for copy in gather_a:
        copy.start()
    for copy in gather_a:
        copy.wait_recv()
    quarter = pl.ds(QUARTER * y, QUARTER)
    gather_y = [remote(prefix.at[quarter], prefix.at[quarter], gy_s.at[j - 1], gy_r.at[j - 1], y_peer(j)) for j in (1, 2, 3)]
    for copy in gather_y:
        copy.start()
    send_columns(SECOND, CHUNKS)

    loads[5].wait()
    for copy in gather_y:
        copy.wait_recv()
    sums[...] = prefix[pl.ds(KSUM, 3)].reshape(24, LANES)
    same = iota((LANES, LANES), 0) // HD == iota((LANES, LANES), 1) // HD
    ones = same.astype(F32).astype(BF16)
    ones = jnp.concatenate([ones, ones], axis=0)

    def two_parts(value):
        high = value.astype(BF16)
        return high, (value - high.astype(F32)).astype(BF16)

    def attend(j, qq):
        qq = jnp.maximum(qq, 0.0)
        tile = prefix[pl.ds(4 * j, 4)].reshape(HD, LANES)
        block = jnp.where(same, jnp.concatenate([tile] * 4, axis=0), 0.0)
        qb = qq.astype(BF16)
        numer = jnp.dot(
            jnp.concatenate([qb, qb], axis=1), jnp.concatenate(two_parts(block), axis=0), preferred_element_type=F32
        )
        denom = jnp.dot(
            jnp.concatenate(two_parts(qq * sums[pl.ds(j, 1), :]), axis=1), ones, preferred_element_type=F32
        )
        return (numer / (denom + EPS)).astype(BF16)

    def attend_step(j, carry):
        out = attend(j, tile_of(q, j))
        att[:, :, :, pl.ds(pl.multiple_of(j * LANES, LANES), LANES)] = out.astype(F32).reshape(2, 8, 8, LANES).astype(BF16)
        return carry

    lax.fori_loop(0, FULL_TILES, attend_step, 0)
    out = attend(FULL_TILES, tail_of(q)).astype(F32)
    att[:, :, :, FULL_TILES * LANES :] = out[:, :TAIL].reshape(2, 8, 8, TAIL).astype(BF16)

    def corners(jc):
        pl.when(c > 0)(lambda: sends[1][1](jc).wait_recv())
        pl.when(c < 7)(lambda: sends[0][1](jc).wait_recv())
        both = jnp.concatenate([col_in[0, jc], col_in[1, jc]], axis=0)
        got = jnp.zeros((32, LANES), F32)
        for t in range(4):
            got = got + jnp.dot(pick[t], both[:, t * LANES : (t + 1) * LANES], preferred_element_type=F32)
        cor_out[0, jc] = got[:16].astype(BF16)
        cor_out[1, jc] = got[16:].astype(BF16)
        pl.when(r > 0)(lambda: up_corner(jc).start())
        pl.when(r < 7)(lambda: down_corner(jc).start())

    def finish(jc):
        pl.when(r < 7)(lambda: up_corner(jc).wait_recv())
        pl.when(r > 0)(lambda: down_corner(jc).wait_recv())
        halves = []
        for t in range(4):
            start = (t // 2) * HU + jc * CHUNK + (t % 2) * LANES
            lanes = pl.ds(pl.multiple_of(start, LANES), LANES)
            part = slice(t * LANES, (t + 1) * LANES)
            rows = jnp.concatenate([col_in[0, jc, :, part], col_in[1, jc, :, part], cor_in[0, jc], cor_in[1, jc]], axis=0)
            laid = jnp.dot(spread[t], rows, preferred_element_type=F32)
            total = conv[:, :, lanes]
            for a in range(3):
                lo = jnp.broadcast_to(w[3 * a : 3 * a + 1, lanes], (8, LANES))
                hi = jnp.broadcast_to(w[3 * a + 2 : 3 * a + 3, lanes], (8, LANES))
                ends = jnp.where(sub == 0, lo, jnp.where(sub == 7, hi, 0.0))
                total = total + laid[a * 128 : (a + 1) * 128].reshape(16, 8, LANES) * ends
            halves.append(total)
        for t in (0, 1):
            value, gate = halves[t], halves[t + 2]
            lanes = pl.ds(pl.multiple_of(jc * CHUNK + t * LANES, LANES), LANES)
            gated[:, :, :, lanes] = (value * (gate / (1.0 + jnp.exp(-gate)))).reshape(2, 8, 8, LANES).astype(BF16)

    corners(0)

    def chunk_step(jc, carry):
        corners(jc)
        finish(jc - 1)
        return carry

    lax.fori_loop(1, CHUNKS, chunk_step, 0)
    finish(CHUNKS - 1)

    pl.when(r > 0)(lambda: up_row.wait_send())
    pl.when(r < 7)(lambda: down_row.wait_send())
    for group in (reduce_y, reduce_a, reduce_b, gather_a, gather_y):
        for copy in group:
            copy.wait_send()
    for b in range(1, 8):
        pl.when(f < b)(lambda b=b: to_later(b).wait_send())

    def drain(jc, carry):
        for ok, copy in sends:
            pl.when(ok)(lambda copy=copy: copy(jc).wait_send())
        pl.when(r > 0)(lambda: up_corner(jc).wait_send())
        pl.when(r < 7)(lambda: down_corner(jc).wait_send())
        return carry

    lax.fori_loop(0, CHUNKS, drain, 0)


def on_device(queries, keys, values, hidden, conv_weight, conv_bias):
    vmem, dma = pltpu.VMEM, pltpu.SemaphoreType.DMA
    units = lambda *n: vmem((*n, 8, LANES), F32)
    scratch = [
        vmem(queries.shape, BF16), vmem(keys.shape, BF16), vmem(values.shape, BF16), vmem(hidden.shape, BF16),
        vmem((9, CH), F32), vmem((1, CH), F32),
        units(UNITS), vmem((24, LANES), F32), units(3, QUARTER), units(QUARTER), units(3, PIECE), units(PIECE),
        units(3, PIECE), units(PIECE), units(8, PIECE), units(UNITS),
        vmem((2, CHUNKS, 16, 2 * CHUNK), BF16), vmem((2, CHUNKS, 16, 2 * CHUNK), BF16), vmem((2, 2, 8, CH), BF16),
        vmem((2, CHUNKS, 16, LANES), BF16), vmem((2, CHUNKS, 16, LANES), BF16),
        vmem((16, 8, CH), F32), vmem((4, 32, 32), BF16), vmem((4, 384, 64), BF16),
        dma((6,)), dma((2,)), dma((2,)), dma((2, CHUNKS)), dma((2, CHUNKS)), dma((2, CHUNKS)), dma((2, CHUNKS)),
        dma((3,)), dma((3,)), dma((3,)), dma((3,)), dma((3,)), dma((3,)), dma((8,)), dma((8,)),
        dma((3,)), dma((3,)), dma((3,)), dma((3,)),
    ]
    return pl.pallas_call(
        kernel,
        out_shape=(
            jax.ShapeDtypeStruct(queries.shape, BF16),
            jax.ShapeDtypeStruct((*hidden.shape[:3], HU), BF16),
        ),
        in_specs=[pl.BlockSpec(memory_space=pl.ANY)] * 6,
        out_specs=[pl.BlockSpec(memory_space=pltpu.VMEM)] * 2,
        scratch_shapes=scratch,
        compiler_params=pltpu.CompilerParams(
            collective_id=0, has_side_effects=True, vmem_limit_bytes=40 * 2**20
        ),
        cost_estimate=pl.CostEstimate(flops=10**8, bytes_accessed=5 * 10**6, transcendentals=360448),
        name="attention_and_convolution",
    )(queries, keys, values, hidden, conv_weight, conv_bias.reshape(1, CH))


def solution(mesh):
    spread = P("frame", "row", "col", None)
    return jax.shard_map(
        on_device,
        mesh=mesh,
        in_specs=(spread, spread, spread, spread, P(), P()),
        out_specs=(spread, spread),
        check_vma=False,
    )
```

```python
import jax
import jax.numpy as jnp
from jax import lax
from jax.experimental import pallas as pl
from jax.experimental.pallas import tpu as pltpu
from jax.sharding import PartitionSpec as P

MESH = pl.DeviceIdType.MESH
F32, BF16 = jnp.float32, jnp.bfloat16

HEADS = 70
HD = 32
WIDTH = HEADS * HD
HU = 2816
CH = 2 * HU
EPS = 1e-6

LANES = 128
FULL_TILES = WIDTH // LANES
TAIL = WIDTH - FULL_TILES * LANES
TILES = FULL_TILES + 1
KSUM = 4 * TILES
UNITS = 80
QUARTER = UNITS // 4
PIECE = QUARTER // 4

CHUNK = 256
CHUNKS = HU // CHUNK
PLAN = ("ooee", "oe", "oecccoce", "oexy", "oexxyy", "ooeeexxxyyy")
WINDOW = 4
CONV = (0, 11, 22, 33, CH // LANES)
LAG = 2
STATE_UNROLL, CONV_UNROLL, TAKE_UNROLL = 17, 2, 4


def iota(shape, dim):
    return lax.broadcasted_iota(jnp.int32, shape, dim)


def kernel(
    q_hbm, k_hbm, v_hbm, h_hbm, w_hbm, b_hbm,
    att_hbm, gated_hbm,
    q, k, v, h, w, bias, att, gated,
    state, sums, y_in, y_sum, za_in, za_sum, zb_in, zb_sum, x_in, prefix,
    col_out, col_in, row_in, cor_out, cor_in, conv, pick, spread,
    local_sem, out_sem, row_s, row_r, col_s, col_r, cor_s, cor_r,
    ry_s, ry_r, ra_s, ra_r, rb_s, rb_r, x_s, x_r, ga_s, ga_r, gy_s, gy_r,
):
    f, r, c = lax.axis_index("frame"), lax.axis_index("row"), lax.axis_index("col")
    y, z = c // 2, (c % 2) * 8 + r
    ia = r % 4

    def y_peer(j):
        return (f, r, ((y + j) % 4) * 2 + c % 2)

    def za_peer(j):
        return (f, (r // 4) * 4 + (ia + j) % 4, c)

    def zb_peer(j):
        far = (z + 4 * j) % 16
        return (f, far % 8, y * 2 + far // 8)

    def remote(src, dst, s, rr, to):
        return pltpu.make_async_remote_copy(
            src_ref=src, dst_ref=dst, send_sem=s, recv_sem=rr, device_id=to, device_id_type=MESH
        )

    loads = [
        pltpu.make_async_copy(src, dst, local_sem.at[n])
        for n, (src, dst) in enumerate(((k_hbm, k), (v_hbm, v), (h_hbm, h), (w_hbm, w), (b_hbm, bias), (q_hbm, q)))
    ]
    for load in loads:
        load.start()

    barrier = pltpu.get_barrier_semaphore()

    def greet(to):
        pl.semaphore_signal(barrier, inc=1, device_id=to, device_id_type=MESH)

    for ok, to in ((c > 0, (f, r, c - 1)), (c < 7, (f, r, c + 1)), (r > 0, (f, r - 1, c)), (r < 7, (f, r + 1, c))):
        pl.when(ok)(lambda to=to: greet(to))
    for j in (1, 2, 3):
        greet(y_peer(j))
        greet(za_peer(j))
        greet(zb_peer(j))
    for j in range(1, 8):
        greet(((f + j) % 8, r, c))

    tok, row = iota((32, 128), 1), iota((32, 128), 0)
    pick_cols = ((tok // 8 == row % 16) & (tok % 8 == jnp.where(row < 16, 0, 7))).astype(F32).astype(BF16)

    def take_columns(jc, carry):
        for half in (0, 1):
            lanes = pl.ds(pl.multiple_of(half * HU + jc * CHUNK, LANES), CHUNK)
            part = h[:, :, :, lanes].astype(F32).reshape(128, CHUNK).astype(BF16)
            got = jnp.dot(pick_cols, part, preferred_element_type=F32).astype(BF16)
            col_out[0, jc, :, half * CHUNK : (half + 1) * CHUNK] = got[:16]
            col_out[1, jc, :, half * CHUNK : (half + 1) * CHUNK] = got[16:]
        return carry

    loads[0].wait()
    loads[1].wait()
    sums[...] = jnp.zeros_like(sums)
    state[pl.ds(KSUM, UNITS - KSUM)] = jnp.zeros((UNITS - KSUM, 8, LANES), F32)
    head_of_lane = iota((HD, LANES), 1) // HD

    def state_tile(j, kk, vv):
        kk = jnp.maximum(kk, 0.0)
        full = lax.dot_general(kk.astype(BF16), vv.astype(BF16), (((0,), (0,)), ((), ())), preferred_element_type=F32)
        tile = jnp.zeros((HD, LANES), F32)
        for g in range(4):
            tile = tile + jnp.where(head_of_lane == g, full[g * HD : (g + 1) * HD], 0.0)
        state[pl.ds(4 * j, 4)] = tile.reshape(4, 8, LANES)
        sums[pl.ds(j, 1), :] = jnp.sum(kk, axis=0, keepdims=True)

    def tail_of(ref):
        part = ref[:, :, :, FULL_TILES * LANES :].astype(F32).reshape(128, TAIL)
        return jnp.concatenate([part, jnp.zeros((128, LANES - TAIL), F32)], axis=1)

    def tile_of(ref, j):
        return ref[:, :, :, pl.ds(pl.multiple_of(j * LANES, LANES), LANES)].astype(F32).reshape(128, LANES)

    def state_step(j, carry):
        state_tile(j, tile_of(k, j), tile_of(v, j))
        return carry

    lax.fori_loop(0, FULL_TILES, state_step, 0, unroll=STATE_UNROLL)
    state_tile(FULL_TILES, tail_of(k), tail_of(v))
    state[pl.ds(KSUM, 3)] = sums[...].reshape(3, 8, LANES)

    @pl.when(c % 2 == 0)
    def _():
        loads[2].wait()
        lax.fori_loop(0, CHUNKS, take_columns, 0, unroll=TAKE_UNROLL)

    peers = 16 + (c > 0).astype(jnp.int32) + (c < 7).astype(jnp.int32) + (r > 0).astype(jnp.int32) + (r < 7).astype(jnp.int32)
    pl.semaphore_wait(barrier, peers)

    reduce_y = [
        remote(state.at[pl.ds(QUARTER * ((y + j) % 4), QUARTER)], y_in.at[j - 1], ry_s.at[j - 1], ry_r.at[j - 1], y_peer(j))
        for j in (1, 2, 3)
    ]
    for copy in reduce_y:
        copy.start()

    sends = (
        (c > 0, lambda jc: remote(col_out.at[0, jc], col_in.at[1, jc], col_s.at[0, jc], col_r.at[1, jc], (f, r, c - 1))),
        (c < 7, lambda jc: remote(col_out.at[1, jc], col_in.at[0, jc], col_s.at[1, jc], col_r.at[0, jc], (f, r, c + 1))),
    )
    up_row = remote(h.at[:, 0], row_in.at[1], row_s.at[0], row_r.at[1], (f, r - 1, c))
    down_row = remote(h.at[:, 7], row_in.at[0], row_s.at[1], row_r.at[0], (f, r + 1, c))

    def up_corner(jc):
        return remote(cor_out.at[0, jc], cor_in.at[1, jc], cor_s.at[0, jc], cor_r.at[1, jc], (f, r - 1, c))

    def down_corner(jc):
        return remote(cor_out.at[1, jc], cor_in.at[0, jc], cor_s.at[1, jc], cor_r.at[0, jc], (f, r + 1, c))

    done = {"e": 0, "o": 0, "x": 0, "y": 0, "c": 0}

    def pump(who):
        jc = done[who]
        for ok, copy in sends:

            @pl.when(ok & (c % 2 == "eo".index(who)))
            def _(copy=copy):
                if jc >= WINDOW:
                    copy(jc - WINDOW).wait_send()
                copy(jc).start()

        done[who] += 1

    def by_parity(even, odd):
        return even if even == odd else jnp.where(c % 2 == 0, even, odd)

    def point(n):
        todo = PLAN[n]
        while todo:
            run = len(todo) - len(todo.lstrip("xy"))
            if run:
                advance(todo[:run].count("x"), todo[:run].count("y"))
            elif todo[0] == "c":
                convolve(1)
            else:
                pump(todo[0])
            todo = todo[max(run, 1) :]

    @pl.when(c % 2 == 1)
    def _():
        loads[2].wait()
        lax.fori_loop(0, CHUNKS, take_columns, 0, unroll=TAKE_UNROLL)

    pl.when(r > 0)(lambda: up_row.start())
    pl.when(r < 7)(lambda: down_row.start())
    point(0)

    @pl.when(c == 0)
    def _():
        col_in[0] = jnp.zeros(col_in.shape[1:], BF16)

    @pl.when(c == 7)
    def _():
        col_in[1] = jnp.zeros(col_in.shape[1:], BF16)

    @pl.when(r == 0)
    def _():
        row_in[0] = jnp.zeros(row_in.shape[1:], BF16)
        cor_in[0] = jnp.zeros(cor_in.shape[1:], BF16)

    @pl.when(r == 7)
    def _():
        row_in[1] = jnp.zeros(row_in.shape[1:], BF16)
        cor_in[1] = jnp.zeros(cor_in.shape[1:], BF16)

    tok, src = iota((128, 64), 0), iota((128, 64), 1)
    tf, tr, tc = tok // 64, (tok // 8) % 8, tok % 8
    side = jnp.where(tc == 7, 1, 0)
    edge = (tc == 0) | (tc == 7)
    for t in range(4):
        for a in range(3):
            at = tr + a - 1
            want = jnp.where(at < 0, 32 + t * 4 + side * 2 + tf, jnp.where(at > 7, 48 + t * 4 + side * 2 + tf, side * 16 + tf * 8 + at))
            spread[t, a * 128 : (a + 1) * 128, :] = (edge & (src == want)).astype(F32).astype(BF16)
    to, frm = iota((32, 32), 0), iota((32, 32), 1)
    for t in range(4):
        o = to % 16
        want = ((o % 4) // 2) * 16 + (o % 2) * 8 + jnp.where(to < 16, 0, 7)
        pick[t] = ((o // 4 == t) & (frm == want)).astype(F32).astype(BF16)

    sub = iota((8, LANES), 0)

    def conv_tile(n, carry):
        lanes = pl.ds(pl.multiple_of(n * LANES, LANES), LANES)
        x = h[:, :, :, lanes].astype(F32)
        above = row_in[0, :, :, lanes].astype(F32)
        below = row_in[1, :, :, lanes].astype(F32)
        x = jnp.concatenate([above[:, None], x, below[:, None]], axis=1)
        wt = [jnp.broadcast_to(w[m : m + 1, lanes], (8, LANES)) for m in range(9)]
        mid, left, right = (jnp.broadcast_to(bias[lanes], (8, LANES)), 0.0, 0.0)
        for a in range(3):
            rows = x[:, a : a + 8]
            left = left + rows * jnp.where(sub == 7, 0.0, wt[3 * a])
            mid = mid + rows * wt[3 * a + 1]
            right = right + rows * jnp.where(sub == 0, 0.0, wt[3 * a + 2])
        left = pltpu.roll(left.reshape(16, 8, LANES), 1, 1)
        right = pltpu.roll(right.reshape(16, 8, LANES), 7, 1)
        conv[:, :, lanes] = mid.reshape(16, 8, LANES) + left + right
        return carry

    def convolve(n):
        if done["c"] == 0:
            loads[3].wait()
            loads[4].wait()
            pl.when(r < 7)(lambda: up_row.wait_recv())
            pl.when(r > 0)(lambda: down_row.wait_recv())
        lax.fori_loop(CONV[done["c"]], CONV[done["c"] + n], conv_tile, 0, unroll=CONV_UNROLL)
        done["c"] += n

    def corners(jc):
        pl.when(c > 0)(lambda: sends[1][1](jc).wait_recv())
        pl.when(c < 7)(lambda: sends[0][1](jc).wait_recv())
        both = jnp.concatenate([col_in[0, jc], col_in[1, jc]], axis=0)
        got = jnp.zeros((32, LANES), F32)
        for t in range(4):
            got = got + jnp.dot(pick[t], both[:, t * LANES : (t + 1) * LANES], preferred_element_type=F32)
        cor_out[0, jc] = got[:16].astype(BF16)
        cor_out[1, jc] = got[16:].astype(BF16)
        pl.when(r > 0)(lambda: up_corner(jc).start())
        pl.when(r < 7)(lambda: down_corner(jc).start())

    def finish(jc):
        pl.when(r < 7)(lambda: up_corner(jc).wait_recv())
        pl.when(r > 0)(lambda: down_corner(jc).wait_recv())
        halves = []
        for t in range(4):
            start = (t // 2) * HU + jc * CHUNK + (t % 2) * LANES
            lanes = pl.ds(pl.multiple_of(start, LANES), LANES)
            part = slice(t * LANES, (t + 1) * LANES)
            rows = jnp.concatenate([col_in[0, jc, :, part], col_in[1, jc, :, part], cor_in[0, jc], cor_in[1, jc]], axis=0)
            laid = jnp.dot(spread[t], rows, preferred_element_type=F32)
            total = conv[:, :, lanes]
            for a in range(3):
                lo = jnp.broadcast_to(w[3 * a : 3 * a + 1, lanes], (8, LANES))
                hi = jnp.broadcast_to(w[3 * a + 2 : 3 * a + 3, lanes], (8, LANES))
                ends = jnp.where(sub == 0, lo, jnp.where(sub == 7, hi, 0.0))
                total = total + laid[a * 128 : (a + 1) * 128].reshape(16, 8, LANES) * ends
            halves.append(total)
        for t in (0, 1):
            value, gate = halves[t], halves[t + 2]
            lanes = pl.ds(pl.multiple_of(jc * CHUNK + t * LANES, LANES), LANES)
            gated[:, :, :, lanes] = (value * (gate / (1.0 + jnp.exp(-gate)))).reshape(2, 8, 8, LANES).astype(BF16)
        gated_out(jc).start()

    def gated_out(jc):
        lanes = pl.ds(pl.multiple_of(jc * CHUNK, LANES), CHUNK)
        return pltpu.make_async_copy(gated.at[:, :, :, lanes], gated_hbm.at[:, :, :, lanes], out_sem.at[jc])

    def chunk_step(jc, carry):
        corners(jc)
        pl.when(jc >= LAG)(lambda: finish(jc - LAG))
        return carry

    def advance(even, odd):
        x, y = done["x"], done["y"]
        lax.fori_loop(by_parity(x, y), by_parity(x + even, y + odd), chunk_step, 0)
        done["x"], done["y"] = x + even, y + odd

    mine = state[pl.ds(QUARTER * y, QUARTER)]
    for j, copy in enumerate(reduce_y):
        copy.wait_recv()
        mine = mine + y_in[j]
    y_sum[...] = mine
    reduce_a = [
        remote(y_sum.at[pl.ds(PIECE * ((ia + j) % 4), PIECE)], za_in.at[j - 1], ra_s.at[j - 1], ra_r.at[j - 1], za_peer(j))
        for j in (1, 2, 3)
    ]
    for copy in reduce_a:
        copy.start()
    point(1)
    mine = y_sum[pl.ds(PIECE * ia, PIECE)]
    for j, copy in enumerate(reduce_a):
        copy.wait_recv()
        mine = mine + za_in[j]
    za_sum[...] = mine
    reduce_b = [remote(za_sum, zb_in.at[j - 1], rb_s.at[j - 1], rb_r.at[j - 1], zb_peer(j)) for j in (1, 2, 3)]
    for copy in reduce_b:
        copy.start()
    point(2)
    mine = za_sum[...]
    for j, copy in enumerate(reduce_b):
        copy.wait_recv()
        mine = mine + zb_in[j]
    zb_sum[...] = mine

    def to_later(b):
        return remote(zb_sum, x_in.at[f], x_s.at[b], x_r.at[f], (b, r, c))

    def from_earlier(b):
        return remote(zb_sum, x_in.at[b], x_s.at[b], x_r.at[b], (b, r, c))

    for b in range(1, 8):
        pl.when(f < b)(lambda b=b: to_later(b).start())
    point(3)

    def add_earlier(b, total):
        from_earlier(b).wait_recv()
        return total + x_in[b]

    here = pl.ds(QUARTER * y + PIECE * ia, PIECE)
    prefix[here] = lax.fori_loop(0, f, add_earlier, zb_sum[...])

    gather_a = [remote(prefix.at[here], prefix.at[here], ga_s.at[j - 1], ga_r.at[j - 1], za_peer(j)) for j in (1, 2, 3)]
    for copy in gather_a:
        copy.start()
    point(4)
    for copy in gather_a:
        copy.wait_recv()
    quarter = pl.ds(QUARTER * y, QUARTER)
    gather_y = [remote(prefix.at[quarter], prefix.at[quarter], gy_s.at[j - 1], gy_r.at[j - 1], y_peer(j)) for j in (1, 2, 3)]
    for copy in gather_y:
        copy.start()
    point(5)

    loads[5].wait()
    for copy in gather_y:
        copy.wait_recv()
    sums[...] = prefix[pl.ds(KSUM, 3)].reshape(24, LANES)
    same = iota((LANES, LANES), 0) // HD == iota((LANES, LANES), 1) // HD
    ones = same.astype(F32).astype(BF16)
    ones = jnp.concatenate([ones, ones], axis=0)

    def two_parts(value):
        high = value.astype(BF16)
        return high, (value - high.astype(F32)).astype(BF16)

    def attend(j, qq):
        qq = jnp.maximum(qq, 0.0)
        tile = prefix[pl.ds(4 * j, 4)].reshape(HD, LANES)
        block = jnp.where(same, jnp.concatenate([tile] * 4, axis=0), 0.0)
        qb = qq.astype(BF16)
        numer = jnp.dot(
            jnp.concatenate([qb, qb], axis=1), jnp.concatenate(two_parts(block), axis=0), preferred_element_type=F32
        )
        denom = jnp.dot(
            jnp.concatenate(two_parts(qq * sums[pl.ds(j, 1), :]), axis=1), ones, preferred_element_type=F32
        )
        return (numer / (denom + EPS)).astype(BF16)

    def attend_step(j, carry):
        out = attend(j, tile_of(q, j))
        att[:, :, :, pl.ds(pl.multiple_of(j * LANES, LANES), LANES)] = out.astype(F32).reshape(2, 8, 8, LANES).astype(BF16)
        return carry

    lax.fori_loop(0, FULL_TILES, attend_step, 0, unroll=STATE_UNROLL)
    out = attend(FULL_TILES, tail_of(q)).astype(F32)
    att[:, :, :, FULL_TILES * LANES :] = out[:, :TAIL].reshape(2, 8, 8, TAIL).astype(BF16)

    att_out = pltpu.make_async_copy(att, att_hbm, out_sem.at[CHUNKS])
    att_out.start()

    for who in "oe":
        while done[who] < CHUNKS:
            pump(who)
    advance(CHUNKS - done["x"], CHUNKS - done["y"])

    def finish_step(jc, carry):
        finish(jc)
        return carry

    lax.fori_loop(CHUNKS - LAG, CHUNKS, finish_step, 0)

    pl.when(r > 0)(lambda: up_row.wait_send())
    pl.when(r < 7)(lambda: down_row.wait_send())
    for group in (reduce_y, reduce_a, reduce_b, gather_a, gather_y):
        for copy in group:
            copy.wait_send()
    for b in range(1, 8):
        pl.when(f < b)(lambda b=b: to_later(b).wait_send())

    def drain(jc, carry):
        gated_out(jc).wait()
        pl.when(r > 0)(lambda: up_corner(jc).wait_send())
        pl.when(r < 7)(lambda: down_corner(jc).wait_send())
        return carry

    lax.fori_loop(0, CHUNKS, drain, 0)
    for jc in range(CHUNKS - WINDOW, CHUNKS):
        for ok, copy in sends:
            pl.when(ok)(lambda copy=copy, jc=jc: copy(jc).wait_send())
    att_out.wait()


def on_device(queries, keys, values, hidden, conv_weight, conv_bias):
    vmem, dma = pltpu.VMEM, pltpu.SemaphoreType.DMA
    units = lambda *n: vmem((*n, 8, LANES), F32)
    scratch = [
        vmem(queries.shape, BF16), vmem(keys.shape, BF16), vmem(values.shape, BF16), vmem(hidden.shape, BF16),
        vmem((9, CH), F32), vmem((CH,), F32), vmem(queries.shape, BF16), vmem((*hidden.shape[:3], HU), BF16),
        units(UNITS), vmem((24, LANES), F32), units(3, QUARTER), units(QUARTER), units(3, PIECE), units(PIECE),
        units(3, PIECE), units(PIECE), units(8, PIECE), units(UNITS),
        vmem((2, CHUNKS, 16, 2 * CHUNK), BF16), vmem((2, CHUNKS, 16, 2 * CHUNK), BF16), vmem((2, 2, 8, CH), BF16),
        vmem((2, CHUNKS, 16, LANES), BF16), vmem((2, CHUNKS, 16, LANES), BF16),
        vmem((16, 8, CH), F32), vmem((4, 32, 32), BF16), vmem((4, 384, 64), BF16),
        dma((6,)), dma((CHUNKS + 1,)), dma((2,)), dma((2,)), dma((2, CHUNKS)), dma((2, CHUNKS)), dma((2, CHUNKS)), dma((2, CHUNKS)),
        dma((3,)), dma((3,)), dma((3,)), dma((3,)), dma((3,)), dma((3,)), dma((8,)), dma((8,)),
        dma((3,)), dma((3,)), dma((3,)), dma((3,)),
    ]
    return pl.pallas_call(
        kernel,
        out_shape=(
            jax.ShapeDtypeStruct(queries.shape, BF16),
            jax.ShapeDtypeStruct((*hidden.shape[:3], HU), BF16),
        ),
        in_specs=[pl.BlockSpec(memory_space=pl.ANY)] * 6,
        out_specs=[pl.BlockSpec(memory_space=pl.ANY)] * 2,
        scratch_shapes=scratch,
        compiler_params=pltpu.CompilerParams(
            collective_id=0, has_side_effects=True, vmem_limit_bytes=62 * 10**6
        ),
        cost_estimate=pl.CostEstimate(flops=10**8, bytes_accessed=5 * 10**6, transcendentals=360448),
        name="attention_and_convolution",
    )(queries, keys, values, hidden, conv_weight, conv_bias)


def solution(mesh):
    spread = P("frame", "row", "col", None)
    return jax.shard_map(
        on_device,
        mesh=mesh,
        in_specs=(spread, spread, spread, spread, P(), P()),
        out_specs=(spread, spread),
        check_vma=False,
    )
```

```python
import jax
import jax.numpy as jnp
from jax import lax
from jax.experimental import pallas as pl
from jax.experimental.pallas import tpu as pltpu
from jax.sharding import PartitionSpec as P

MESH = pl.DeviceIdType.MESH
F32, BF16 = jnp.float32, jnp.bfloat16

HEADS = 70
HD = 32
WIDTH = HEADS * HD
HU = 2816
CH = 2 * HU
EPS = 1e-6

LANES = 128
FULL_TILES = WIDTH // LANES
TAIL = WIDTH - FULL_TILES * LANES
TILES = FULL_TILES + 1
KSUM = 4 * TILES
UNITS = 80
QUARTER = UNITS // 4
PIECE = QUARTER // 4

CHUNK = 256
CHUNKS = HU // CHUNK
PLAN = ("ppp", "pp", "pcpcpcc", "p", "pa", "aa")
SPLIT = 8
WINDOW = 4
CONV = (0, 11, 22, 33, CH // LANES)
LAG = 3
STATE_UNROLL, CONV_UNROLL, TAKE_UNROLL = 17, 2, 4


def iota(shape, dim):
    return lax.broadcasted_iota(jnp.int32, shape, dim)


def kernel(
    q_hbm, k_hbm, v_hbm, h_hbm, w_hbm, b_hbm,
    att_hbm, gated_hbm,
    q, k, v, h, w, bias, att, gated,
    state, sums, y_in, y_sum, za_in, za_sum, zb_in, zb_sum, x_in, prefix,
    col_out, col_in, row_in, cor_out, cor_in, conv, pick, spread,
    local_sem, out_sem, row_s, row_r, col_s, col_r, cor_s, cor_r,
    ry_s, ry_r, ra_s, ra_r, rb_s, rb_r, x_s, x_r, ga_s, ga_r, gy_s, gy_r,
):
    f, r, c = lax.axis_index("frame"), lax.axis_index("row"), lax.axis_index("col")
    y, z = c // 2, (c % 2) * 8 + r
    ia = r % 4

    def y_peer(j):
        return (f, r, ((y + j) % 4) * 2 + c % 2)

    def za_peer(j):
        return (f, (r // 4) * 4 + (ia + j) % 4, c)

    def zb_peer(j):
        far = (z + 4 * j) % 16
        return (f, far % 8, y * 2 + far // 8)

    def remote(src, dst, s, rr, to):
        return pltpu.make_async_remote_copy(
            src_ref=src, dst_ref=dst, send_sem=s, recv_sem=rr, device_id=to, device_id_type=MESH
        )

    loads = [
        pltpu.make_async_copy(src, dst, local_sem.at[n])
        for n, (src, dst) in enumerate(((k_hbm, k), (v_hbm, v), (h_hbm, h), (w_hbm, w), (b_hbm, bias), (q_hbm, q)))
    ]
    for load in loads:
        load.start()

    barrier = pltpu.get_barrier_semaphore()

    def greet(to):
        pl.semaphore_signal(barrier, inc=1, device_id=to, device_id_type=MESH)

    for ok, to in ((c > 0, (f, r, c - 1)), (c < 7, (f, r, c + 1)), (r > 0, (f, r - 1, c)), (r < 7, (f, r + 1, c))):
        pl.when(ok)(lambda to=to: greet(to))
    for j in (1, 2, 3):
        greet(y_peer(j))
        greet(za_peer(j))
        greet(zb_peer(j))
    for j in range(1, 8):
        greet(((f + j) % 8, r, c))

    tok, row = iota((32, 128), 1), iota((32, 128), 0)
    pick_cols = ((tok // 8 == row % 16) & (tok % 8 == jnp.where(row < 16, 0, 7))).astype(F32).astype(BF16)

    def take_columns(jc, carry):
        for half in (0, 1):
            lanes = pl.ds(pl.multiple_of(half * HU + jc * CHUNK, LANES), CHUNK)
            part = h[:, :, :, lanes].astype(F32).reshape(128, CHUNK).astype(BF16)
            got = jnp.dot(pick_cols, part, preferred_element_type=F32).astype(BF16)
            col_out[0, jc, :, half * CHUNK : (half + 1) * CHUNK] = got[:16]
            col_out[1, jc, :, half * CHUNK : (half + 1) * CHUNK] = got[16:]
        return carry

    loads[0].wait()
    loads[1].wait()
    sums[...] = jnp.zeros_like(sums)
    state[pl.ds(KSUM, UNITS - KSUM)] = jnp.zeros((UNITS - KSUM, 8, LANES), F32)
    head_of_lane = iota((HD, LANES), 1) // HD

    def state_tile(j, kk, vv):
        kk = jnp.maximum(kk, 0.0)
        full = lax.dot_general(kk.astype(BF16), vv.astype(BF16), (((0,), (0,)), ((), ())), preferred_element_type=F32)
        tile = jnp.zeros((HD, LANES), F32)
        for g in range(4):
            tile = tile + jnp.where(head_of_lane == g, full[g * HD : (g + 1) * HD], 0.0)
        state[pl.ds(4 * j, 4)] = tile.reshape(4, 8, LANES)
        sums[pl.ds(j, 1), :] = jnp.sum(kk, axis=0, keepdims=True)

    def tail_of(ref):
        part = ref[:, :, :, FULL_TILES * LANES :].astype(F32).reshape(128, TAIL)
        return jnp.concatenate([part, jnp.zeros((128, LANES - TAIL), F32)], axis=1)

    def tile_of(ref, j):
        return ref[:, :, :, pl.ds(pl.multiple_of(j * LANES, LANES), LANES)].astype(F32).reshape(128, LANES)

    def state_step(j, carry):
        state_tile(j, tile_of(k, j), tile_of(v, j))
        return carry

    lax.fori_loop(0, FULL_TILES, state_step, 0, unroll=STATE_UNROLL)
    state_tile(FULL_TILES, tail_of(k), tail_of(v))
    state[pl.ds(KSUM, 3)] = sums[...].reshape(3, 8, LANES)

    @pl.when(c % 2 == 0)
    def _():
        loads[2].wait()
        lax.fori_loop(0, CHUNKS, take_columns, 0, unroll=TAKE_UNROLL)

    peers = 16 + (c > 0).astype(jnp.int32) + (c < 7).astype(jnp.int32) + (r > 0).astype(jnp.int32) + (r < 7).astype(jnp.int32)
    pl.semaphore_wait(barrier, peers)

    reduce_y = [
        remote(state.at[pl.ds(QUARTER * ((y + j) % 4), QUARTER)], y_in.at[j - 1], ry_s.at[j - 1], ry_r.at[j - 1], y_peer(j))
        for j in (1, 2, 3)
    ]
    for copy in reduce_y:
        copy.start()

    sends = (
        (c > 0, lambda jc: remote(col_out.at[0, jc], col_in.at[1, jc], col_s.at[0, jc], col_r.at[1, jc], (f, r, c - 1))),
        (c < 7, lambda jc: remote(col_out.at[1, jc], col_in.at[0, jc], col_s.at[1, jc], col_r.at[0, jc], (f, r, c + 1))),
    )
    up_row = remote(h.at[:, 0], row_in.at[1], row_s.at[0], row_r.at[1], (f, r - 1, c))
    down_row = remote(h.at[:, 7], row_in.at[0], row_s.at[1], row_r.at[0], (f, r + 1, c))

    def up_corner(jc):
        return remote(cor_out.at[0, jc], cor_in.at[1, jc], cor_s.at[0, jc], cor_r.at[1, jc], (f, r - 1, c))

    def down_corner(jc):
        return remote(cor_out.at[1, jc], cor_in.at[0, jc], cor_s.at[1, jc], cor_r.at[0, jc], (f, r + 1, c))

    done = {"p": 0, "a": 0, "c": 0}

    def pump(n):
        for jc in range(done["p"], done["p"] + n):
            for ok, copy in sends:

                @pl.when(ok)
                def _(copy=copy):
                    if jc >= WINDOW:
                        copy(jc - WINDOW).wait_send()
                    copy(jc).start()

        done["p"] += n

    def point(n):
        for what in PLAN[n]:
            if what == "p":
                pump(1)
            elif what == "a":
                advance(1)
            else:
                convolve(1)

    pl.when(c % 2 == 1)(lambda: loads[2].wait())
    pl.when(r > 0)(lambda: up_row.start())
    pl.when(r < 7)(lambda: down_row.start())

    def take_if_odd(first, last):
        @pl.when(c % 2 == 1)
        def _():
            lax.fori_loop(first, last, take_columns, 0, unroll=TAKE_UNROLL)

    take_if_odd(0, len(PLAN[0]))
    point(0)
    take_if_odd(len(PLAN[0]), CHUNKS)

    @pl.when(c == 0)
    def _():
        col_in[0] = jnp.zeros(col_in.shape[1:], BF16)

    @pl.when(c == 7)
    def _():
        col_in[1] = jnp.zeros(col_in.shape[1:], BF16)

    @pl.when(r == 0)
    def _():
        row_in[0] = jnp.zeros(row_in.shape[1:], BF16)
        cor_in[0] = jnp.zeros(cor_in.shape[1:], BF16)

    @pl.when(r == 7)
    def _():
        row_in[1] = jnp.zeros(row_in.shape[1:], BF16)
        cor_in[1] = jnp.zeros(cor_in.shape[1:], BF16)

    tok, src = iota((128, 64), 0), iota((128, 64), 1)
    tf, tr, tc = tok // 64, (tok // 8) % 8, tok % 8
    side = jnp.where(tc == 7, 1, 0)
    edge = (tc == 0) | (tc == 7)
    for t in range(4):
        for a in range(3):
            at = tr + a - 1
            want = jnp.where(at < 0, 32 + t * 4 + side * 2 + tf, jnp.where(at > 7, 48 + t * 4 + side * 2 + tf, side * 16 + tf * 8 + at))
            spread[t, a * 128 : (a + 1) * 128, :] = (edge & (src == want)).astype(F32).astype(BF16)
    to, frm = iota((32, LANES), 0), iota((32, LANES), 1)
    o = to % 16
    want = ((o % 4) // 2) * 16 + (o % 2) * 8 + jnp.where(to < 16, 0, 7)
    pick[...] = ((o // 4 == frm // 32) & (frm % 32 == want)).astype(F32).astype(BF16)

    sub = iota((8, LANES), 0)

    def conv_tile(n, carry):
        lanes = pl.ds(pl.multiple_of(n * LANES, LANES), LANES)
        x = h[:, :, :, lanes].astype(F32)
        above = row_in[0, :, :, lanes].astype(F32)
        below = row_in[1, :, :, lanes].astype(F32)
        x = jnp.concatenate([above[:, None], x, below[:, None]], axis=1)
        wt = [jnp.broadcast_to(w[m : m + 1, lanes], (8, LANES)) for m in range(9)]
        mid, left, right = (jnp.broadcast_to(bias[lanes], (8, LANES)), 0.0, 0.0)
        for a in range(3):
            rows = x[:, a : a + 8]
            left = left + rows * jnp.where(sub == 7, 0.0, wt[3 * a])
            mid = mid + rows * wt[3 * a + 1]
            right = right + rows * jnp.where(sub == 0, 0.0, wt[3 * a + 2])
        left = pltpu.roll(left.reshape(16, 8, LANES), 1, 1)
        right = pltpu.roll(right.reshape(16, 8, LANES), 7, 1)
        conv[:, :, lanes] = mid.reshape(16, 8, LANES) + left + right
        return carry

    def convolve(n):
        if done["c"] == 0:
            loads[3].wait()
            loads[4].wait()
            pl.when(r < 7)(lambda: up_row.wait_recv())
            pl.when(r > 0)(lambda: down_row.wait_recv())
        lax.fori_loop(CONV[done["c"]], CONV[done["c"] + n], conv_tile, 0, unroll=CONV_UNROLL)
        done["c"] += n

    def corners(jc):
        pl.when(c > 0)(lambda: sends[1][1](jc).wait_recv())
        pl.when(c < 7)(lambda: sends[0][1](jc).wait_recv())
        both = jnp.concatenate([col_in[0, jc], col_in[1, jc]], axis=0)
        tiles = jnp.concatenate([both[:, t * LANES : (t + 1) * LANES] for t in range(4)], axis=0)
        got = jnp.dot(pick[...], tiles, preferred_element_type=F32)
        cor_out[0, jc] = got[:16].astype(BF16)
        cor_out[1, jc] = got[16:].astype(BF16)
        pl.when(r > 0)(lambda: up_corner(jc).start())
        pl.when(r < 7)(lambda: down_corner(jc).start())

    def finish(jc):
        pl.when(r < 7)(lambda: up_corner(jc).wait_recv())
        pl.when(r > 0)(lambda: down_corner(jc).wait_recv())
        halves = []
        for t in range(4):
            start = (t // 2) * HU + jc * CHUNK + (t % 2) * LANES
            lanes = pl.ds(pl.multiple_of(start, LANES), LANES)
            part = slice(t * LANES, (t + 1) * LANES)
            rows = jnp.concatenate([col_in[0, jc, :, part], col_in[1, jc, :, part], cor_in[0, jc], cor_in[1, jc]], axis=0)
            laid = jnp.dot(spread[t], rows, preferred_element_type=F32)
            total = conv[:, :, lanes]
            for a in range(3):
                lo = jnp.broadcast_to(w[3 * a : 3 * a + 1, lanes], (8, LANES))
                hi = jnp.broadcast_to(w[3 * a + 2 : 3 * a + 3, lanes], (8, LANES))
                ends = jnp.where(sub == 0, lo, jnp.where(sub == 7, hi, 0.0))
                total = total + laid[a * 128 : (a + 1) * 128].reshape(16, 8, LANES) * ends
            halves.append(total)
        for t in (0, 1):
            value, gate = halves[t], halves[t + 2]
            lanes = pl.ds(pl.multiple_of(jc * CHUNK + t * LANES, LANES), LANES)
            gated[:, :, :, lanes] = (value * (gate / (1.0 + jnp.exp(-gate)))).reshape(2, 8, 8, LANES).astype(BF16)
        gated_out(jc).start()

    def gated_out(jc):
        lanes = pl.ds(pl.multiple_of(jc * CHUNK, LANES), CHUNK)
        return pltpu.make_async_copy(gated.at[:, :, :, lanes], gated_hbm.at[:, :, :, lanes], out_sem.at[jc])

    def chunk_step(jc, carry):
        corners(jc)
        pl.when(jc >= LAG)(lambda: finish(jc - LAG))
        return carry

    def advance(n):
        lax.fori_loop(done["a"], done["a"] + n, chunk_step, 0)
        done["a"] += n

    mine = state[pl.ds(QUARTER * y, QUARTER)]
    for j, copy in enumerate(reduce_y):
        copy.wait_recv()
        mine = mine + y_in[j]
    y_sum[...] = mine
    reduce_a = [
        remote(y_sum.at[pl.ds(PIECE * ((ia + j) % 4), PIECE)], za_in.at[j - 1], ra_s.at[j - 1], ra_r.at[j - 1], za_peer(j))
        for j in (1, 2, 3)
    ]
    for copy in reduce_a:
        copy.start()
    point(1)
    mine = y_sum[pl.ds(PIECE * ia, PIECE)]
    for j, copy in enumerate(reduce_a):
        copy.wait_recv()
        mine = mine + za_in[j]
    za_sum[...] = mine
    reduce_b = [remote(za_sum, zb_in.at[j - 1], rb_s.at[j - 1], rb_r.at[j - 1], zb_peer(j)) for j in (1, 2, 3)]
    for copy in reduce_b:
        copy.start()
    point(2)
    mine = za_sum[...]
    for j, copy in enumerate(reduce_b):
        copy.wait_recv()
        mine = mine + zb_in[j]
    zb_sum[...] = mine

    def to_later(b):
        return remote(zb_sum, x_in.at[f], x_s.at[b], x_r.at[f], (b, r, c))

    def from_earlier(b):
        return remote(zb_sum, x_in.at[b], x_s.at[b], x_r.at[b], (b, r, c))

    for b in range(1, 8):
        pl.when(f < b)(lambda b=b: to_later(b).start())
    point(3)

    def add_earlier(b, total):
        from_earlier(b).wait_recv()
        return total + x_in[b]

    here = pl.ds(QUARTER * y + PIECE * ia, PIECE)
    prefix[here] = lax.fori_loop(0, f, add_earlier, zb_sum[...])

    gather_a = [remote(prefix.at[here], prefix.at[here], ga_s.at[j - 1], ga_r.at[j - 1], za_peer(j)) for j in (1, 2, 3)]
    for copy in gather_a:
        copy.start()
    point(4)
    for copy in gather_a:
        copy.wait_recv()
    quarter = pl.ds(QUARTER * y, QUARTER)
    gather_y = [remote(prefix.at[quarter], prefix.at[quarter], gy_s.at[j - 1], gy_r.at[j - 1], y_peer(j)) for j in (1, 2, 3)]
    for copy in gather_y:
        copy.start()
    point(5)

    ahead = done["p"] - done["a"]

    def chunk_and_send(jc, carry):
        corners(jc)

        @pl.when(jc + ahead < CHUNKS)
        def _():
            for ok, copy in sends:

                @pl.when(ok)
                def _(copy=copy):
                    copy(jc + ahead - WINDOW).wait_send()
                    copy(jc + ahead).start()

        pl.when(jc >= LAG)(lambda: finish(jc - LAG))
        return carry

    lax.fori_loop(done["a"], SPLIT, chunk_and_send, 0)

    loads[5].wait()
    for copy in gather_y:
        copy.wait_recv()
    sums[...] = prefix[pl.ds(KSUM, 3)].reshape(24, LANES)
    same = iota((LANES, LANES), 0) // HD == iota((LANES, LANES), 1) // HD
    ones = same.astype(F32).astype(BF16)
    ones = jnp.concatenate([ones, ones], axis=0)

    def two_parts(value):
        high = value.astype(BF16)
        return high, (value - high.astype(F32)).astype(BF16)

    def attend(j, qq):
        qq = jnp.maximum(qq, 0.0)
        tile = prefix[pl.ds(4 * j, 4)].reshape(HD, LANES)
        block = jnp.where(same, jnp.concatenate([tile] * 4, axis=0), 0.0)
        qb = qq.astype(BF16)
        numer = jnp.dot(
            jnp.concatenate([qb, qb], axis=1), jnp.concatenate(two_parts(block), axis=0), preferred_element_type=F32
        )
        denom = jnp.dot(
            jnp.concatenate(two_parts(qq * sums[pl.ds(j, 1), :]), axis=1), ones, preferred_element_type=F32
        )
        return (numer / (denom + EPS)).astype(BF16)

    def attend_step(j, carry):
        out = attend(j, tile_of(q, j))
        att[:, :, :, pl.ds(pl.multiple_of(j * LANES, LANES), LANES)] = out.astype(F32).reshape(2, 8, 8, LANES).astype(BF16)
        return carry

    lax.fori_loop(0, FULL_TILES, attend_step, 0, unroll=STATE_UNROLL)
    out = attend(FULL_TILES, tail_of(q)).astype(F32)
    att[:, :, :, FULL_TILES * LANES :] = out[:, :TAIL].reshape(2, 8, 8, TAIL).astype(BF16)

    att_out = pltpu.make_async_copy(att, att_hbm, out_sem.at[CHUNKS])
    att_out.start()

    lax.fori_loop(SPLIT, CHUNKS, chunk_and_send, 0)

    def finish_step(jc, carry):
        finish(jc)
        return carry

    lax.fori_loop(CHUNKS - LAG, CHUNKS, finish_step, 0)

    pl.when(r > 0)(lambda: up_row.wait_send())
    pl.when(r < 7)(lambda: down_row.wait_send())
    for group in (reduce_y, reduce_a, reduce_b, gather_a, gather_y):
        for copy in group:
            copy.wait_send()
    for b in range(1, 8):
        pl.when(f < b)(lambda b=b: to_later(b).wait_send())

    def drain(jc, carry):
        gated_out(jc).wait()
        pl.when(r > 0)(lambda: up_corner(jc).wait_send())
        pl.when(r < 7)(lambda: down_corner(jc).wait_send())
        return carry

    lax.fori_loop(0, CHUNKS, drain, 0)
    for jc in range(CHUNKS - WINDOW, CHUNKS):
        for ok, copy in sends:
            pl.when(ok)(lambda copy=copy, jc=jc: copy(jc).wait_send())
    att_out.wait()


def on_device(queries, keys, values, hidden, conv_weight, conv_bias):
    vmem, dma = pltpu.VMEM, pltpu.SemaphoreType.DMA
    units = lambda *n: vmem((*n, 8, LANES), F32)
    scratch = [
        vmem(queries.shape, BF16), vmem(keys.shape, BF16), vmem(values.shape, BF16), vmem(hidden.shape, BF16),
        vmem((9, CH), F32), vmem((CH,), F32), vmem(queries.shape, BF16), vmem((*hidden.shape[:3], HU), BF16),
        units(UNITS), vmem((24, LANES), F32), units(3, QUARTER), units(QUARTER), units(3, PIECE), units(PIECE),
        units(3, PIECE), units(PIECE), units(8, PIECE), units(UNITS),
        vmem((2, CHUNKS, 16, 2 * CHUNK), BF16), vmem((2, CHUNKS, 16, 2 * CHUNK), BF16), vmem((2, 2, 8, CH), BF16),
        vmem((2, CHUNKS, 16, LANES), BF16), vmem((2, CHUNKS, 16, LANES), BF16),
        vmem((16, 8, CH), F32), vmem((32, LANES), BF16), vmem((4, 384, 64), BF16),
        dma((6,)), dma((CHUNKS + 1,)), dma((2,)), dma((2,)), dma((2, CHUNKS)), dma((2, CHUNKS)), dma((2, CHUNKS)), dma((2, CHUNKS)),
        dma((3,)), dma((3,)), dma((3,)), dma((3,)), dma((3,)), dma((3,)), dma((8,)), dma((8,)),
        dma((3,)), dma((3,)), dma((3,)), dma((3,)),
    ]
    return pl.pallas_call(
        kernel,
        out_shape=(
            jax.ShapeDtypeStruct(queries.shape, BF16),
            jax.ShapeDtypeStruct((*hidden.shape[:3], HU), BF16),
        ),
        in_specs=[pl.BlockSpec(memory_space=pl.ANY)] * 6,
        out_specs=[pl.BlockSpec(memory_space=pl.ANY)] * 2,
        scratch_shapes=scratch,
        compiler_params=pltpu.CompilerParams(
            collective_id=0, has_side_effects=True, vmem_limit_bytes=62 * 10**6
        ),
        cost_estimate=pl.CostEstimate(flops=10**8, bytes_accessed=5 * 10**6, transcendentals=360448),
        name="attention_and_convolution",
    )(queries, keys, values, hidden, conv_weight, conv_bias)


def solution(mesh):
    spread = P("frame", "row", "col", None)
    return jax.shard_map(
        on_device,
        mesh=mesh,
        in_specs=(spread, spread, spread, spread, P(), P()),
        out_specs=(spread, spread),
        check_vma=False,
    )
```

```python
import jax
import jax.numpy as jnp
from jax import lax
from jax.experimental import pallas as pl
from jax.experimental.pallas import tpu as pltpu
from jax.sharding import PartitionSpec as P

MESH = pl.DeviceIdType.MESH
F32, BF16 = jnp.float32, jnp.bfloat16

HEADS = 70
HD = 32
WIDTH = HEADS * HD
HU = 2816
CH = 2 * HU
EPS = 1e-6

LANES = 128
FULL_TILES = WIDTH // LANES
TAIL = WIDTH - FULL_TILES * LANES
TILES = FULL_TILES + 1
KSUM = 4 * TILES
UNITS = 80
QUARTER = UNITS // 4
PIECE = QUARTER // 4

CHUNK = 256
CHUNKS = HU // CHUNK
PLAN = ("ppp", "pp", "pcpcpcc", "p", "pa", "aa")
SPLIT = 8
WINDOW = 4
CONV = (0, 11, 22, 33, CH // LANES)
LAG = 3
STATE_UNROLL, CONV_UNROLL, TAKE_UNROLL = 17, 2, 4


def iota(shape, dim):
    return lax.broadcasted_iota(jnp.int32, shape, dim)


def kernel(
    q_hbm, k_hbm, v_hbm, h_hbm, w_hbm, b_hbm,
    att_hbm, gated_hbm,
    q, k, v, h, w, bias, att, gated,
    state, sums, y_in, y_sum, za_in, za_sum, zb_in, zb_sum, x_in, prefix,
    col_out, col_in, row_in, cor_out, cor_in, conv, pick, spread,
    local_sem, out_sem, row_s, row_r, col_s, col_r, cor_s, cor_r,
    ry_s, ry_r, ra_s, ra_r, rb_s, rb_r, x_s, x_r, ga_s, ga_r, gy_s, gy_r,
):
    f, r, c = lax.axis_index("frame"), lax.axis_index("row"), lax.axis_index("col")
    y, z = c // 2, (c % 2) * 8 + r
    ia = r % 4

    def y_peer(j):
        return (f, r, ((y + j) % 4) * 2 + c % 2)

    def za_peer(j):
        return (f, (r // 4) * 4 + (ia + j) % 4, c)

    def zb_peer(j):
        far = (z + 4 * j) % 16
        return (f, far % 8, y * 2 + far // 8)

    def remote(src, dst, s, rr, to):
        return pltpu.make_async_remote_copy(
            src_ref=src, dst_ref=dst, send_sem=s, recv_sem=rr, device_id=to, device_id_type=MESH
        )

    loads = [
        pltpu.make_async_copy(src, dst, local_sem.at[n])
        for n, (src, dst) in enumerate(((k_hbm, k), (v_hbm, v), (h_hbm, h), (w_hbm, w), (b_hbm, bias), (q_hbm, q)))
    ]
    for load in loads:
        load.start()

    barrier = pltpu.get_barrier_semaphore()

    def greet(to):
        pl.semaphore_signal(barrier, inc=1, device_id=to, device_id_type=MESH)

    for ok, to in ((c > 0, (f, r, c - 1)), (c < 7, (f, r, c + 1)), (r == 4, (f, r - 1, c)), (r == 3, (f, r + 1, c))):
        pl.when(ok)(lambda to=to: greet(to))
    for j in (1, 2, 3):
        greet(y_peer(j))
        greet(za_peer(j))
        if j != 2:
            greet(zb_peer(j))
    for j in range(1, 8):
        greet(((f + j) % 8, r, c))

    tok, row = iota((32, 128), 1), iota((32, 128), 0)
    pick_cols = ((tok // 8 == row % 16) & (tok % 8 == jnp.where(row < 16, 0, 7))).astype(F32).astype(BF16)

    def take_columns(jc, carry):
        for half in (0, 1):
            lanes = pl.ds(pl.multiple_of(half * HU + jc * CHUNK, LANES), CHUNK)
            part = h[:, :, :, lanes].astype(F32).reshape(128, CHUNK).astype(BF16)
            got = jnp.dot(pick_cols, part, preferred_element_type=F32).astype(BF16)
            col_out[0, jc, :, half * CHUNK : (half + 1) * CHUNK] = got[:16]
            col_out[1, jc, :, half * CHUNK : (half + 1) * CHUNK] = got[16:]
        return carry

    loads[0].wait()
    loads[1].wait()
    sums[...] = jnp.zeros_like(sums)
    state[pl.ds(KSUM, UNITS - KSUM)] = jnp.zeros((UNITS - KSUM, 8, LANES), F32)
    head_of_lane = iota((HD, LANES), 1) // HD

    def state_tile(j, kk, vv):
        kk = jnp.maximum(kk, 0.0)
        full = lax.dot_general(kk.astype(BF16), vv.astype(BF16), (((0,), (0,)), ((), ())), preferred_element_type=F32)
        tile = jnp.zeros((HD, LANES), F32)
        for g in range(4):
            tile = tile + jnp.where(head_of_lane == g, full[g * HD : (g + 1) * HD], 0.0)
        state[pl.ds(4 * j, 4)] = tile.reshape(4, 8, LANES)
        sums[pl.ds(j, 1), :] = jnp.sum(kk, axis=0, keepdims=True)

    def tail_of(ref):
        part = ref[:, :, :, FULL_TILES * LANES :].astype(F32).reshape(128, TAIL)
        return jnp.concatenate([part, jnp.zeros((128, LANES - TAIL), F32)], axis=1)

    def tile_of(ref, j):
        return ref[:, :, :, pl.ds(pl.multiple_of(j * LANES, LANES), LANES)].astype(F32).reshape(128, LANES)

    def state_step(j, carry):
        state_tile(j, tile_of(k, j), tile_of(v, j))
        return carry

    lax.fori_loop(0, FULL_TILES, state_step, 0, unroll=STATE_UNROLL)
    state_tile(FULL_TILES, tail_of(k), tail_of(v))
    state[pl.ds(KSUM, 3)] = sums[...].reshape(3, 8, LANES)

    @pl.when(c % 2 == 0)
    def _():
        loads[2].wait()
        lax.fori_loop(0, CHUNKS, take_columns, 0, unroll=TAKE_UNROLL)

    peers = 15 + (c > 0).astype(jnp.int32) + (c < 7).astype(jnp.int32) + ((r == 3) | (r == 4)).astype(jnp.int32)
    pl.semaphore_wait(barrier, peers)

    reduce_y = [
        remote(state.at[pl.ds(QUARTER * ((y + j) % 4), QUARTER)], y_in.at[j - 1], ry_s.at[j - 1], ry_r.at[j - 1], y_peer(j))
        for j in (1, 2, 3)
    ]
    for copy in reduce_y:
        copy.start()

    sends = (
        (c > 0, lambda jc: remote(col_out.at[0, jc], col_in.at[1, jc], col_s.at[0, jc], col_r.at[1, jc], (f, r, c - 1))),
        (c < 7, lambda jc: remote(col_out.at[1, jc], col_in.at[0, jc], col_s.at[1, jc], col_r.at[0, jc], (f, r, c + 1))),
    )
    up_row = remote(h.at[:, 0], row_in.at[1], row_s.at[0], row_r.at[1], (f, r - 1, c))
    down_row = remote(h.at[:, 7], row_in.at[0], row_s.at[1], row_r.at[0], (f, r + 1, c))

    def up_corner(jc):
        return remote(cor_out.at[0, jc], cor_in.at[1, jc], cor_s.at[0, jc], cor_r.at[1, jc], (f, r - 1, c))

    def down_corner(jc):
        return remote(cor_out.at[1, jc], cor_in.at[0, jc], cor_s.at[1, jc], cor_r.at[0, jc], (f, r + 1, c))

    done = {"p": 0, "a": 0, "c": 0}

    def pump(n):
        for jc in range(done["p"], done["p"] + n):
            for ok, copy in sends:

                @pl.when(ok)
                def _(copy=copy):
                    if jc >= WINDOW:
                        copy(jc - WINDOW).wait_send()
                    copy(jc).start()

        done["p"] += n

    def point(n):
        for what in PLAN[n]:
            if what == "p":
                pump(1)
            elif what == "a":
                advance(1)
            else:
                convolve(1)

    pl.when(c % 2 == 1)(lambda: loads[2].wait())
    pl.when(r > 0)(lambda: up_row.start())
    pl.when(r < 7)(lambda: down_row.start())

    def take_if_odd(first, last):
        @pl.when(c % 2 == 1)
        def _():
            lax.fori_loop(first, last, take_columns, 0, unroll=TAKE_UNROLL)

    take_if_odd(0, len(PLAN[0]))
    point(0)
    take_if_odd(len(PLAN[0]), CHUNKS)

    @pl.when(c == 0)
    def _():
        col_in[0] = jnp.zeros(col_in.shape[1:], BF16)

    @pl.when(c == 7)
    def _():
        col_in[1] = jnp.zeros(col_in.shape[1:], BF16)

    @pl.when(r == 0)
    def _():
        row_in[0] = jnp.zeros(row_in.shape[1:], BF16)
        cor_in[0] = jnp.zeros(cor_in.shape[1:], BF16)

    @pl.when(r == 7)
    def _():
        row_in[1] = jnp.zeros(row_in.shape[1:], BF16)
        cor_in[1] = jnp.zeros(cor_in.shape[1:], BF16)

    tok, src = iota((128, 64), 0), iota((128, 64), 1)
    tf, tr, tc = tok // 64, (tok // 8) % 8, tok % 8
    side = jnp.where(tc == 7, 1, 0)
    edge = (tc == 0) | (tc == 7)
    for t in range(4):
        for a in range(3):
            at = tr + a - 1
            want = jnp.where(at < 0, 32 + t * 4 + side * 2 + tf, jnp.where(at > 7, 48 + t * 4 + side * 2 + tf, side * 16 + tf * 8 + at))
            spread[t, a * 128 : (a + 1) * 128, :] = (edge & (src == want)).astype(F32).astype(BF16)
    to, frm = iota((32, LANES), 0), iota((32, LANES), 1)
    o = to % 16
    want = ((o % 4) // 2) * 16 + (o % 2) * 8 + jnp.where(to < 16, 0, 7)
    pick[...] = ((o // 4 == frm // 32) & (frm % 32 == want)).astype(F32).astype(BF16)

    sub = iota((8, LANES), 0)

    def conv_tile(n, carry):
        lanes = pl.ds(pl.multiple_of(n * LANES, LANES), LANES)
        x = h[:, :, :, lanes].astype(F32)
        above = row_in[0, :, :, lanes].astype(F32)
        below = row_in[1, :, :, lanes].astype(F32)
        x = jnp.concatenate([above[:, None], x, below[:, None]], axis=1)
        wt = [jnp.broadcast_to(w[m : m + 1, lanes], (8, LANES)) for m in range(9)]
        mid, left, right = (jnp.broadcast_to(bias[lanes], (8, LANES)), 0.0, 0.0)
        for a in range(3):
            rows = x[:, a : a + 8]
            left = left + rows * jnp.where(sub == 7, 0.0, wt[3 * a])
            mid = mid + rows * wt[3 * a + 1]
            right = right + rows * jnp.where(sub == 0, 0.0, wt[3 * a + 2])
        left = pltpu.roll(left.reshape(16, 8, LANES), 1, 1)
        right = pltpu.roll(right.reshape(16, 8, LANES), 7, 1)
        conv[:, :, lanes] = mid.reshape(16, 8, LANES) + left + right
        return carry

    def convolve(n):
        if done["c"] == 0:
            loads[3].wait()
            loads[4].wait()
            pl.when(r < 7)(lambda: up_row.wait_recv())
            pl.when(r > 0)(lambda: down_row.wait_recv())
        lax.fori_loop(CONV[done["c"]], CONV[done["c"] + n], conv_tile, 0, unroll=CONV_UNROLL)
        done["c"] += n

    def corners(jc):
        pl.when(c > 0)(lambda: sends[1][1](jc).wait_recv())
        pl.when(c < 7)(lambda: sends[0][1](jc).wait_recv())
        both = jnp.concatenate([col_in[0, jc], col_in[1, jc]], axis=0)
        tiles = jnp.concatenate([both[:, t * LANES : (t + 1) * LANES] for t in range(4)], axis=0)
        got = jnp.dot(pick[...], tiles, preferred_element_type=F32)
        cor_out[0, jc] = got[:16].astype(BF16)
        cor_out[1, jc] = got[16:].astype(BF16)
        pl.when(r > 0)(lambda: up_corner(jc).start())
        pl.when(r < 7)(lambda: down_corner(jc).start())

    def finish(jc):
        pl.when(r < 7)(lambda: up_corner(jc).wait_recv())
        pl.when(r > 0)(lambda: down_corner(jc).wait_recv())
        halves = []
        for t in range(4):
            start = (t // 2) * HU + jc * CHUNK + (t % 2) * LANES
            lanes = pl.ds(pl.multiple_of(start, LANES), LANES)
            part = slice(t * LANES, (t + 1) * LANES)
            rows = jnp.concatenate([col_in[0, jc, :, part], col_in[1, jc, :, part], cor_in[0, jc], cor_in[1, jc]], axis=0)
            laid = jnp.dot(spread[t], rows, preferred_element_type=F32)
            total = conv[:, :, lanes]
            for a in range(3):
                lo = jnp.broadcast_to(w[3 * a : 3 * a + 1, lanes], (8, LANES))
                hi = jnp.broadcast_to(w[3 * a + 2 : 3 * a + 3, lanes], (8, LANES))
                ends = jnp.where(sub == 0, lo, jnp.where(sub == 7, hi, 0.0))
                total = total + laid[a * 128 : (a + 1) * 128].reshape(16, 8, LANES) * ends
            halves.append(total)
        for t in (0, 1):
            value, gate = halves[t], halves[t + 2]
            lanes = pl.ds(pl.multiple_of(jc * CHUNK + t * LANES, LANES), LANES)
            gated[:, :, :, lanes] = (value * (gate / (1.0 + jnp.exp(-gate)))).reshape(2, 8, 8, LANES).astype(BF16)
        gated_out(jc).start()

    def gated_out(jc):
        lanes = pl.ds(pl.multiple_of(jc * CHUNK, LANES), CHUNK)
        return pltpu.make_async_copy(gated.at[:, :, :, lanes], gated_hbm.at[:, :, :, lanes], out_sem.at[jc])

    def chunk_step(jc, carry):
        corners(jc)
        pl.when(jc >= LAG)(lambda: finish(jc - LAG))
        return carry

    def advance(n):
        lax.fori_loop(done["a"], done["a"] + n, chunk_step, 0)
        done["a"] += n

    mine = state[pl.ds(QUARTER * y, QUARTER)]
    for j, copy in enumerate(reduce_y):
        copy.wait_recv()
        mine = mine + y_in[j]
    y_sum[...] = mine
    reduce_a = [
        remote(y_sum.at[pl.ds(PIECE * ((ia + j) % 4), PIECE)], za_in.at[j - 1], ra_s.at[j - 1], ra_r.at[j - 1], za_peer(j))
        for j in (1, 2, 3)
    ]
    for copy in reduce_a:
        copy.start()
    point(1)
    mine = y_sum[pl.ds(PIECE * ia, PIECE)]
    for j, copy in enumerate(reduce_a):
        copy.wait_recv()
        mine = mine + za_in[j]
    za_sum[...] = mine
    reduce_b = [remote(za_sum, zb_in.at[j - 1], rb_s.at[j - 1], rb_r.at[j - 1], zb_peer(j)) for j in (1, 2, 3)]
    for copy in reduce_b:
        copy.start()
    point(2)
    mine = za_sum[...]
    for j, copy in enumerate(reduce_b):
        copy.wait_recv()
        mine = mine + zb_in[j]
    zb_sum[...] = mine

    def to_later(b):
        return remote(zb_sum, x_in.at[f], x_s.at[b], x_r.at[f], (b, r, c))

    def from_earlier(b):
        return remote(zb_sum, x_in.at[b], x_s.at[b], x_r.at[b], (b, r, c))

    for b in range(1, 8):
        pl.when(f < b)(lambda b=b: to_later(b).start())
    point(3)

    def add_earlier(b, total):
        from_earlier(b).wait_recv()
        return total + x_in[b]

    here = pl.ds(QUARTER * y + PIECE * ia, PIECE)
    prefix[here] = lax.fori_loop(0, f, add_earlier, zb_sum[...])

    gather_a = [remote(prefix.at[here], prefix.at[here], ga_s.at[j - 1], ga_r.at[j - 1], za_peer(j)) for j in (1, 2, 3)]
    for copy in gather_a:
        copy.start()
    point(4)
    for copy in gather_a:
        copy.wait_recv()
    quarter = pl.ds(QUARTER * y, QUARTER)
    gather_y = [remote(prefix.at[quarter], prefix.at[quarter], gy_s.at[j - 1], gy_r.at[j - 1], y_peer(j)) for j in (1, 2, 3)]
    for copy in gather_y:
        copy.start()
    point(5)

    ahead = done["p"] - done["a"]

    def chunk_and_send(jc, carry):
        corners(jc)

        @pl.when(jc + ahead < CHUNKS)
        def _():
            for ok, copy in sends:

                @pl.when(ok)
                def _(copy=copy):
                    copy(jc + ahead - WINDOW).wait_send()
                    copy(jc + ahead).start()

        pl.when(jc >= LAG)(lambda: finish(jc - LAG))
        return carry

    lax.fori_loop(done["a"], SPLIT, chunk_and_send, 0)

    loads[5].wait()
    for copy in gather_y:
        copy.wait_recv()
    sums[...] = prefix[pl.ds(KSUM, 3)].reshape(24, LANES)
    same = iota((LANES, LANES), 0) // HD == iota((LANES, LANES), 1) // HD
    ones = same.astype(F32).astype(BF16)
    ones = jnp.concatenate([ones, ones], axis=0)

    def two_parts(value):
        high = value.astype(BF16)
        return high, (value - high.astype(F32)).astype(BF16)

    def attend(j, qq):
        qq = jnp.maximum(qq, 0.0)
        tile = prefix[pl.ds(4 * j, 4)].reshape(HD, LANES)
        block = jnp.where(same, jnp.concatenate([tile] * 4, axis=0), 0.0)
        qb = qq.astype(BF16)
        numer = jnp.dot(
            jnp.concatenate([qb, qb], axis=1), jnp.concatenate(two_parts(block), axis=0), preferred_element_type=F32
        )
        denom = jnp.dot(
            jnp.concatenate(two_parts(qq * sums[pl.ds(j, 1), :]), axis=1), ones, preferred_element_type=F32
        )
        return (numer / (denom + EPS)).astype(BF16)

    def attend_step(j, carry):
        out = attend(j, tile_of(q, j))
        att[:, :, :, pl.ds(pl.multiple_of(j * LANES, LANES), LANES)] = out.astype(F32).reshape(2, 8, 8, LANES).astype(BF16)
        return carry

    lax.fori_loop(0, FULL_TILES, attend_step, 0, unroll=STATE_UNROLL)
    out = attend(FULL_TILES, tail_of(q)).astype(F32)
    att[:, :, :, FULL_TILES * LANES :] = out[:, :TAIL].reshape(2, 8, 8, TAIL).astype(BF16)

    att_out = pltpu.make_async_copy(att, att_hbm, out_sem.at[CHUNKS])
    att_out.start()

    lax.fori_loop(SPLIT, CHUNKS, chunk_and_send, 0)

    def finish_step(jc, carry):
        finish(jc)
        return carry

    lax.fori_loop(CHUNKS - LAG, CHUNKS, finish_step, 0)

    pl.when(r > 0)(lambda: up_row.wait_send())
    pl.when(r < 7)(lambda: down_row.wait_send())
    for group in (reduce_y, reduce_a, reduce_b, gather_a, gather_y):
        for copy in group:
            copy.wait_send()
    for b in range(1, 8):
        pl.when(f < b)(lambda b=b: to_later(b).wait_send())

    def drain(jc, carry):
        gated_out(jc).wait()
        pl.when(r > 0)(lambda: up_corner(jc).wait_send())
        pl.when(r < 7)(lambda: down_corner(jc).wait_send())
        return carry

    lax.fori_loop(0, CHUNKS, drain, 0)
    for jc in range(CHUNKS - WINDOW, CHUNKS):
        for ok, copy in sends:
            pl.when(ok)(lambda copy=copy, jc=jc: copy(jc).wait_send())
    att_out.wait()


def on_device(queries, keys, values, hidden, conv_weight, conv_bias):
    vmem, dma = pltpu.VMEM, pltpu.SemaphoreType.DMA
    units = lambda *n: vmem((*n, 8, LANES), F32)
    scratch = [
        vmem(queries.shape, BF16), vmem(keys.shape, BF16), vmem(values.shape, BF16), vmem(hidden.shape, BF16),
        vmem((9, CH), F32), vmem((CH,), F32), vmem(queries.shape, BF16), vmem((*hidden.shape[:3], HU), BF16),
        units(UNITS), vmem((24, LANES), F32), units(3, QUARTER), units(QUARTER), units(3, PIECE), units(PIECE),
        units(3, PIECE), units(PIECE), units(8, PIECE), units(UNITS),
        vmem((2, CHUNKS, 16, 2 * CHUNK), BF16), vmem((2, CHUNKS, 16, 2 * CHUNK), BF16), vmem((2, 2, 8, CH), BF16),
        vmem((2, CHUNKS, 16, LANES), BF16), vmem((2, CHUNKS, 16, LANES), BF16),
        vmem((16, 8, CH), F32), vmem((32, LANES), BF16), vmem((4, 384, 64), BF16),
        dma((6,)), dma((CHUNKS + 1,)), dma((2,)), dma((2,)), dma((2, CHUNKS)), dma((2, CHUNKS)), dma((2, CHUNKS)), dma((2, CHUNKS)),
        dma((3,)), dma((3,)), dma((3,)), dma((3,)), dma((3,)), dma((3,)), dma((8,)), dma((8,)),
        dma((3,)), dma((3,)), dma((3,)), dma((3,)),
    ]
    return pl.pallas_call(
        kernel,
        out_shape=(
            jax.ShapeDtypeStruct(queries.shape, BF16),
            jax.ShapeDtypeStruct((*hidden.shape[:3], HU), BF16),
        ),
        in_specs=[pl.BlockSpec(memory_space=pl.ANY)] * 6,
        out_specs=[pl.BlockSpec(memory_space=pl.ANY)] * 2,
        scratch_shapes=scratch,
        compiler_params=pltpu.CompilerParams(
            collective_id=0, has_side_effects=True, vmem_limit_bytes=62 * 10**6
        ),
        cost_estimate=pl.CostEstimate(flops=10**8, bytes_accessed=5 * 10**6, transcendentals=360448),
        name="attention_and_convolution",
    )(queries, keys, values, hidden, conv_weight, conv_bias)


def solution(mesh):
    spread = P("frame", "row", "col", None)
    return jax.shard_map(
        on_device,
        mesh=mesh,
        in_specs=(spread, spread, spread, spread, P(), P()),
        out_specs=(spread, spread),
        check_vma=False,
    )
```
